256 devices in a mesh: dp: 32 (over y, z), tensor: 8 (over x, core).
Axes of the slice: x: 4, y: 4, z: 8, core: 2. Of those that a mesh axis runs over, the one named last changes fastest.
Arguments:
- inputs: bfloat16 [4096, 1152], P('dp'), may hold values from -20 to 20
- gate_weight: bfloat16 [1152, 6912], P(None, 'tensor'), may hold values from -0.1875 to 0.1875
- up_weight: bfloat16 [1152, 6912], P(None, 'tensor'), may hold values from -1 to 1
- down_weight: bfloat16 [1152, 6912], P(None, 'tensor'), may hold values from -1 to 1
- out_grad: bfloat16 [4096, 1152], P('dp'), may hold values from -1 to 1
- later_norms: float32 [32], P('dp'), may hold values from 0.1 to 10
Outputs:
- input_grad: bfloat16 [4096, 1152], P(('dp', 'tensor'))
- gate_grad: float32 [1152, 6912], P('dp', 'tensor')
- up_grad: float32 [1152, 6912], P('dp', 'tensor')
- down_grad: float32 [1152, 6912], P('dp', 'tensor')
The draws below stay inside these ranges and needn't reach their ends.
All inputs are finite; a program needn't handle non-finite values.
Results may differ from the reference program's by a relative error of at most 0.0049.
Values sent between devices are 32-bit elements; how exact they have to be, the bound alone decides.
No kernel may reach another device: no remote copies, remote signals or barrier semaphores. Data moves between devices by JAX's collectives and lax.ppermute only.
A program may use at most 128 MiB of HBM per device.

```python
import math
import jax
import jax.numpy as jnp
from jax import lax

D = 1152
FF = 6912
SEQ = 128
EXAMPLES = 32


def correlated(key, common_mix, noise_mix, low, high):
    keys = jax.random.split(key, 3)
    common = jnp.clip(jax.random.normal(keys[0], (EXAMPLES, 1, D), jnp.float32), -4.0, 4.0)
    noise = jnp.clip(jax.random.normal(keys[1], (EXAMPLES, SEQ, D), jnp.float32), -4.0, 4.0)
    spread = jnp.exp(jax.random.uniform(keys[2], (EXAMPLES, SEQ, 1), jnp.float32, math.log(low), math.log(high)))
    return (spread * (common_mix * common + noise_mix * noise)).reshape(EXAMPLES * SEQ, D)


def ramped(key, fan_in):
    base = jnp.clip(jax.random.normal(key, (D, FF), jnp.float32), -4.0, 4.0) / math.sqrt(fan_in)
    column_ramp = 3.0 ** (jnp.arange(FF, dtype=jnp.float32) / max(FF - 1, 1) - 0.5)
    return base * column_ramp[None, :]


def draw_inputs(key, part):
    key = jax.random.fold_in(key, 1)
    mixed = correlated(key, 0.6, 0.8, 0.3, 3.0)
    return mixed.astype(jnp.bfloat16)


def draw_out_grad(key, part):
    key = jax.random.fold_in(key, 2)
    factor = 3.0 / math.sqrt(SEQ * D * FF)
    mixed = correlated(key, 0.6, 0.8, 0.3, 3.0)
    return (factor * mixed).astype(jnp.bfloat16)


def draw_up_weight(key, part):
    key = jax.random.fold_in(key, 3)
    return ramped(key, D).astype(jnp.bfloat16)


def draw_down_weight(key, part):
    key = jax.random.fold_in(key, 4)
    return ramped(key, FF).astype(jnp.bfloat16)


def block_levels(own_key, dims, cuts, least, top_value):
    factor_of = 1.0
    for position, shards_of in cuts:
        draws = jax.random.uniform(jax.random.fold_in(jax.random.fold_in(own_key, 6), position), (shards_of,), jnp.float32, least / len(cuts), top_value / len(cuts))
        factor_of = factor_of * jnp.repeat(jnp.exp(draws), dims[position] // shards_of).reshape((-1,) + (1,) * (len(dims) - 1 - position))
    return factor_of


def gaussian(stream_key, shape, width, bound, cuts=(), kind=jnp.bfloat16):
    drawn = jax.random.normal(stream_key, shape, jnp.float32) * width
    if len(cuts) > 0:
        drawn = block_levels(stream_key, shape, cuts, -0.22, 0.18) * drawn
    return jnp.clip(drawn, min=-bound, max=bound).astype(kind)


def setup_inputs(seed: int = 0) -> dict:
    splits = jax.random.split(jax.random.key(seed), 7)
    inputs = draw_inputs(jax.random.fold_in(splits[6], 71), 0)
    gate_weight = gaussian(splits[1], (D, FF), D ** -0.5, 0.1875, ((1, 8),))
    up_weight = draw_up_weight(jax.random.fold_in(splits[6], 71), 0)
    down_weight = draw_down_weight(jax.random.fold_in(splits[6], 71), 0)
    out_grad = draw_out_grad(jax.random.fold_in(splits[6], 71), 0)
    later_norms = jnp.clip(jnp.exp(math.log(10.0) - 4.6051702 * jax.random.uniform(splits[5], (EXAMPLES,), jnp.float32) ** block_levels(splits[5], (EXAMPLES,), ((0, 32),), -0.2, 0.2)), 0.1, 10.0)
    return dict(inputs=inputs, gate_weight=gate_weight, up_weight=up_weight, down_weight=down_weight, out_grad=out_grad, later_norms=later_norms)


CLIP_NORM = 1.8
GELU_C = 0.7978845608028654

def gelu_parts(pre):
    tangent = jnp.tanh(GELU_C * (pre + 0.044715 * pre * pre * pre))
    activated = 0.5 * pre * (1.0 + tangent)
    gelu_slope = 0.5 * (1.0 + tangent) + 0.5 * pre * (1.0 - tangent * tangent) * GELU_C * (1.0 + 3.0 * 0.044715 * pre * pre)
    return (activated, gelu_slope)

def gram_matrix(block):
    wide = block.astype(jnp.float32)
    return jnp.dot(wide, wide.T, preferred_element_type=jnp.float32)

def example_norm(pieces):
    x_block, gate_block, up_block, dy_block, hid_block = pieces
    input_gram = gram_matrix(x_block)
    first = jnp.sum(input_gram * (gram_matrix(gate_block) + gram_matrix(up_block)))
    second = jnp.sum(gram_matrix(dy_block) * gram_matrix(hid_block))
    return first + second

def reference(inputs, gate_weight, up_weight, down_weight, out_grad, later_norms):
    gate_pre = jnp.dot(inputs, gate_weight, preferred_element_type=jnp.float32)
    up_pre = jnp.dot(inputs, up_weight, preferred_element_type=jnp.float32)
    activated, gelu_slope = gelu_parts(gate_pre)
    hidden = (activated * up_pre).astype(jnp.bfloat16)
    hidden_grad = jnp.dot(out_grad, down_weight, preferred_element_type=jnp.float32)
    gate_back = (hidden_grad * up_pre * gelu_slope).astype(jnp.bfloat16)
    up_back = (hidden_grad * activated).astype(jnp.bfloat16)
    input_grad = (jnp.dot(gate_back, gate_weight.T, preferred_element_type=jnp.float32) + jnp.dot(up_back, up_weight.T, preferred_element_type=jnp.float32)).astype(jnp.bfloat16)
    own = lax.map(example_norm, (inputs.reshape(EXAMPLES, SEQ, D), gate_back.reshape(EXAMPLES, SEQ, FF), up_back.reshape(EXAMPLES, SEQ, FF), out_grad.reshape(EXAMPLES, SEQ, D), hidden.reshape(EXAMPLES, SEQ, FF)))
    clip_factor = jnp.minimum(1.0, CLIP_NORM / jnp.sqrt(later_norms + own))
    token_weight = jnp.repeat(clip_factor * math.sqrt(D * FF / EXAMPLES), SEQ)[:, None]
    weighted_gate = (gate_back * token_weight).astype(jnp.bfloat16)
    weighted_up = (up_back * token_weight).astype(jnp.bfloat16)
    weighted_hidden = (hidden * token_weight).astype(jnp.bfloat16)
    gate_grad = jnp.dot(inputs.T, weighted_gate, preferred_element_type=jnp.float32)
    up_grad = jnp.dot(inputs.T, weighted_up, preferred_element_type=jnp.float32)
    down_grad = jnp.dot(out_grad.T, weighted_hidden, preferred_element_type=jnp.float32)
    return (input_grad, gate_grad, up_grad, down_grad)
```

```python
import math

import jax
import jax.numpy as jnp
from jax import lax
from jax.experimental import pallas as pl
from jax.experimental.pallas import tpu as pltpu
from jax.sharding import Mesh, PartitionSpec as P

CLIP_NORM = 1.8
GELU_C = 0.7978845608028654
NY, NZ, NX, NC = 4, 8, 4, 2
VMEM_LIMIT = 48 * 1024 * 1024
F32 = jnp.float32
BF16 = jnp.bfloat16


def gelu_parts(pre):
    tangent = jnp.tanh(GELU_C * (pre + 0.044715 * pre * pre * pre))
    activated = 0.5 * pre * (1.0 + tangent)
    gelu_slope = 0.5 * (1.0 + tangent) + 0.5 * pre * (1.0 - tangent * tangent) * GELU_C * (
        1.0 + 3.0 * 0.044715 * pre * pre
    )
    return (activated, gelu_slope)


def shift(array, axis, step):
    size = lax.axis_size(axis)
    return lax.ppermute(array, axis, [(i, (i + step) % size) for i in range(size)])


def dot(left, right, dims):
    return lax.dot_general(left, right, (dims, ((), ())), preferred_element_type=F32)


def own_kernel(x_ref, dy_ref, wg_ref, wu_ref, wd_ref, g_ref, u_ref, h_ref, own_ref):
    x = x_ref[...]
    dy = dy_ref[...]
    g, u, h = forward(x, dy, wg_ref[...], wu_ref[...], wd_ref[...])
    g_ref[...] = g
    u_ref[...] = u
    h_ref[...] = h
    own = jnp.sum(gram(x) * (gram(g) + gram(u)) + gram(dy) * gram(h))
    own_ref[...] = jnp.full(own_ref.shape, own, F32)


def group_kernel(
    place_ref, scale_ref, x_ref, dy_ref, g_ref, u_ref, h_ref, *refs
):
    got_refs, swap_refs = refs[: NY - 1], refs[NY - 1 : 2 * NY - 2]
    wg_ref, wu_ref, wd_ref, out_ref, xs, dys, x_part, dy_part = refs[2 * NY - 2 :]
    tokens, width = x_ref.shape
    others = NY - 1
    part = width // NY
    first = place_ref[0] == 0
    for e in range(others):
        rows = slice(e * tokens, (e + 1) * tokens)
        a, b = got_refs[e][...], swap_refs[e][...]
        xs[rows, :] = jnp.where(first, a, b).astype(BF16)
        dys[rows, :] = jnp.where(first, b, a).astype(BF16)
    for k in range(NY):
        @pl.when(place_ref[1] == k)
        def _():
            cols = slice(k * part, (k + 1) * part)
            x_part[:tokens, :] = x_ref[:, cols]
            dy_part[:tokens, :] = dy_ref[:, cols]
            x_part[tokens:, :] = xs[:, cols]
            dy_part[tokens:, :] = dys[:, cols]
    g, u, h = forward(xs[...], dys[...], wg_ref[...], wu_ref[...], wd_ref[...])
    rows = part // NZ
    for m, (left, mine, other) in enumerate(
        ((x_part, g_ref, g), (x_part, u_ref, u), (dy_part, h_ref, h))
    ):
        scaled = [(mine[...].astype(F32) * scale_ref[0, 0:1, 0:1]).astype(BF16)]
        for e in range(others):
            piece = other[e * tokens : (e + 1) * tokens].astype(F32)
            scaled.append((piece * scale_ref[e + 1, 0:1, 0:1]).astype(BF16))
        grad = dot(left[...], jnp.concatenate(scaled, axis=0), ((0,), (0,)))
        for z in range(NZ):
            out_ref[z, m * rows : (m + 1) * rows, :] = grad[z * rows : (z + 1) * rows]


def forward(x, dy, gate_weight, up_weight, down_weight):
    gate_pre = dot(x, gate_weight, ((1,), (0,)))
    up_pre = dot(x, up_weight, ((1,), (0,)))
    activated, gelu_slope = gelu_parts(gate_pre)
    hidden = (activated * up_pre).astype(BF16)
    hidden_grad = dot(dy, down_weight, ((1,), (0,)))
    gate_back = (hidden_grad * up_pre * gelu_slope).astype(BF16)
    up_back = (hidden_grad * activated).astype(BF16)
    return gate_back, up_back, hidden


def gram(matrix):
    return dot(matrix, matrix, ((1,), (1,)))


def per_device(inputs, gate_weight, up_weight, down_weight, out_grad, later_norms):
    y = lax.axis_index("y")
    x = lax.axis_index("x")
    core = lax.axis_index("core")
    tokens, width = inputs.shape
    ff = gate_weight.shape[1]
    weights = (gate_weight, up_weight, down_weight)
    vmem = pl.BlockSpec(memory_space=pltpu.VMEM)
    params = pltpu.CompilerParams(vmem_limit_bytes=VMEM_LIMIT)

    mine = jnp.where(core == 0, inputs, out_grad).astype(F32)
    got = [shift(mine, "y", k) for k in (1, 3, 2)]

    hidden_type = jax.ShapeDtypeStruct((tokens, ff), BF16)
    gate_back, up_back, hidden, own = pl.pallas_call(
        own_kernel,
        out_shape=[hidden_type, hidden_type, hidden_type, jax.ShapeDtypeStruct((8, 128), F32)],
        in_specs=[vmem] * 5,
        out_specs=[vmem] * 4,
        compiler_params=params,
        name="own_example",
    )(inputs, out_grad, *weights)
    own = own + shift(own, "core", 1)
    own = own + (shift(own, "x", 1) + shift(own, "x", 3)) + shift(own, "x", 2)
    clip = jnp.minimum(1.0, CLIP_NORM / jnp.sqrt(later_norms[:, None] + own))
    scale = clip * math.sqrt(width * ff * NX * NC / (NY * NZ))
    scales = jnp.stack([scale] + [shift(scale, "y", k) for k in (1, 3, 2)])

    swapped = [shift(a, "core", 1) for a in got]
    part = width // NY
    grads = pl.pallas_call(
        group_kernel,
        out_shape=jax.ShapeDtypeStruct((NZ, 3 * part // NZ, ff), F32),
        in_specs=[pl.BlockSpec(memory_space=pltpu.SMEM)] + [vmem] * (6 + 2 * (NY - 1) + 3),
        out_specs=vmem,
        scratch_shapes=[
            pltpu.VMEM(((NY - 1) * tokens, width), BF16),
            pltpu.VMEM(((NY - 1) * tokens, width), BF16),
            pltpu.VMEM((NY * tokens, part), BF16),
            pltpu.VMEM((NY * tokens, part), BF16),
        ],
        compiler_params=params,
        name="group_gradients",
    )(
        jnp.stack([core, y]).astype(jnp.int32), scales, inputs, out_grad, gate_back, up_back, hidden,
        *got, *swapped, *weights,
    )
    grads = lax.psum_scatter(grads, "z", scatter_dimension=0, tiled=False)
    rows = part // NZ

    partial = dot(gate_back, gate_weight, ((1,), (1,))) + dot(up_back, up_weight, ((1,), (1,)))
    partial = partial.reshape(NX, NC, tokens // (NX * NC), width)
    keep = lax.dynamic_index_in_dim(partial, core, 1, False)
    give = lax.dynamic_index_in_dim(partial, 1 - core, 1, False)
    keep = keep + shift(give, "core", 1)
    total = lax.dynamic_index_in_dim(keep, x, 0, False)
    for k in (1, 3, 2):
        total = total + shift(lax.dynamic_index_in_dim(keep, (x + k) % NX, 0, False), "x", k)
    return (total.astype(BF16), grads[:rows], grads[rows : 2 * rows], grads[2 * rows :])


def solution(mesh):
    fine = Mesh(mesh.devices.reshape(NY, NZ, NX, NC), ("y", "z", "x", "core"))
    dp, tensor = ("y", "z"), ("x", "core")
    in_specs = (
        P(dp, None),
        P(None, tensor),
        P(None, tensor),
        P(None, tensor),
        P(dp, None),
        P(dp),
    )
    out_specs = (P(dp + tensor, None), P(dp, tensor), P(dp, tensor), P(dp, tensor))
    return jax.shard_map(
        per_device, mesh=fine, in_specs=in_specs, out_specs=out_specs, check_vma=False
    )
```

```python
import functools
import math

import jax
import jax.numpy as jnp
from jax import lax
from jax.experimental import pallas as pl
from jax.experimental.pallas import tpu as pltpu
from jax.sharding import Mesh, PartitionSpec as P

CLIP_NORM = 1.8
GELU_C = 0.7978845608028654
NY, NZ, NX, NC = 4, 8, 4, 2
OWN_MIB = 48
F32 = jnp.float32
BF16 = jnp.bfloat16


def gelu_parts(pre):
    tangent = jnp.tanh(GELU_C * (pre + 0.044715 * pre * pre * pre))
    activated = 0.5 * pre * (1.0 + tangent)
    gelu_slope = 0.5 * (1.0 + tangent) + 0.5 * pre * (1.0 - tangent * tangent) * GELU_C * (
        1.0 + 3.0 * 0.044715 * pre * pre
    )
    return (activated, gelu_slope)


def shift(array, axis, step):
    size = lax.axis_size(axis)
    return lax.ppermute(array, axis, [(i, (i + step) % size) for i in range(size)])


def dot(left, right, dims):
    return lax.dot_general(left, right, (dims, ((), ())), preferred_element_type=F32)


def forward(x, dy, gate_weight, up_weight, down_weight):
    gate_pre = dot(x, gate_weight, ((1,), (1,)))
    up_pre = dot(x, up_weight, ((1,), (1,)))
    activated, gelu_slope = gelu_parts(gate_pre)
    hidden = (activated * up_pre).astype(BF16)
    hidden_grad = dot(dy, down_weight, ((1,), (1,)))
    gate_back = (hidden_grad * up_pre * gelu_slope).astype(BF16)
    up_back = (hidden_grad * activated).astype(BF16)
    return gate_back, up_back, hidden


def gram(matrix):
    return dot(matrix, matrix, ((1,), (1,)))


def prepare_kernel(x_ref, dy_ref, out_ref, token_ref):
    token_ref[...] = jnp.zeros(token_ref.shape, F32)
    first = lax.axis_index("core") == 0

    @pl.when(first)
    def _():
        out_ref[...] = x_ref[...].astype(F32)

    @pl.when(jnp.logical_not(first))
    def _():
        out_ref[...] = dy_ref[...].astype(F32)


def own_kernel(
    x_hbm, dy_hbm, wg_hbm, wu_hbm, wd_hbm, token_ref, g_ref, u_ref, h_ref, keep_ref, give_ref, wg, wu, wd,
    x_ref, dy_ref, rows_ref, sems,
):
    pairs = ((x_hbm, x_ref), (wg_hbm, wg), (wu_hbm, wu), (dy_hbm, dy_ref), (wd_hbm, wd))
    copies = [pltpu.make_async_copy(a, b, sems.at[i]) for i, (a, b) in enumerate(pairs)]
    for copy in copies:
        copy.start()
    copies[0].wait()
    x = x_ref[...]
    gram_x = gram(x)
    copies[1].wait()
    gate_pre = dot(x, wg[...], ((1,), (1,)))
    activated, gelu_slope = gelu_parts(gate_pre)
    copies[2].wait()
    up_pre = dot(x, wu[...], ((1,), (1,)))
    h = (activated * up_pre).astype(BF16)
    copies[3].wait()
    dy = dy_ref[...]
    gram_dy = gram(dy)
    copies[4].wait()
    hidden_grad = dot(dy, wd[...], ((1,), (1,)))
    g = (hidden_grad * up_pre * gelu_slope).astype(BF16)
    u = (hidden_grad * activated).astype(BF16)
    g_ref[...] = g
    u_ref[...] = u
    h_ref[...] = h
    own = jnp.sum(gram_x * (gram(g) + gram(u)) + gram_dy * gram(h))
    total = dot(g, wg[...], ((1,), (0,))) + dot(u, wu[...], ((1,), (0,)))
    rows_ref[...] = total.reshape(rows_ref.shape)
    core = lax.axis_index("core")
    for i in range(NX):
        keep_ref[i] = rows_ref[NC * i + core]
        give_ref[i] = rows_ref[NC * i + 1 - core]
    for ref in (keep_ref, give_ref):
        ref[NX] = jnp.full(ref.shape[1:], own, F32)


def spread_kernel(keep_ref, got_ref, mine_ref, out1, out3, out2, rows_ref):
    rows_ref[...] = keep_ref[...] + got_ref[...]
    x = lax.axis_index("x")
    size = rows_ref.shape[1]
    for step, out_ref in ((0, mine_ref), (1, out1), (3, out3), (2, out2)):
        out_ref[:size, :] = rows_ref[lax.rem(x + step, NX)]
        out_ref[size:, :] = rows_ref[NX, :8, :]


def gather_kernel(mine_ref, got1, got3, got2, later_ref, input_ref, scale_ref, *, factor):
    total = mine_ref[...] + (got1[...] + got3[...]) + got2[...]
    size = input_ref.shape[0]
    input_ref[...] = total[:size].astype(BF16)
    own = total[size:, :128]
    scale_ref[...] = jnp.minimum(1.0, CLIP_NORM / jnp.sqrt(later_ref[0] + own)) * factor


def order_kernel(array_ref, token_ref, out_ref):
    pass


def after(array, token):
    return pl.pallas_call(
        order_kernel,
        out_shape=jax.ShapeDtypeStruct(array.shape, array.dtype),
        in_specs=[pl.BlockSpec(memory_space=pl.ANY)] * 2,
        out_specs=pl.BlockSpec(memory_space=pl.ANY),
        input_output_aliases={0: 0},
        compiler_params=pltpu.CompilerParams(vmem_limit_bytes=1024 * 1024),
        name="order",
    )(array, token)


def merge(got_refs, swap_refs, xs, dys):
    first = lax.axis_index("core") == 0
    row = 0
    for got_ref, swap_ref in zip(got_refs, swap_refs):
        rows = slice(row, row + got_ref.shape[0])
        row += got_ref.shape[0]

        @pl.when(first)
        def _():
            xs[rows, :] = got_ref[...].astype(BF16)
            dys[rows, :] = swap_ref[...].astype(BF16)

        @pl.when(jnp.logical_not(first))
        def _():
            xs[rows, :] = swap_ref[...].astype(BF16)
            dys[rows, :] = got_ref[...].astype(BF16)


def take_part(source_ref, target_ref, offset):
    tokens, width = source_ref.shape
    part = width // NY
    y = lax.axis_index("y")
    for k in range(NY):

        @pl.when(y == k)
        def _():
            target_ref[offset : offset + tokens, :] = source_ref[:, k * part : (k + 1) * part]


def pair_kernel(
    got0, got1, swap0, swap1, wg_ref, wu_ref, wd_ref, g_ref, u_ref, h_ref, xp_ref, dyp_ref, xs, dys
):
    merge((got0, got1), (swap0, swap1), xs, dys)
    take_part(xs, xp_ref, 0)
    take_part(dys, dyp_ref, 0)
    g, u, h = forward(xs[...], dys[...], wg_ref[...], wu_ref[...], wd_ref[...])
    g_ref[...] = g
    u_ref[...] = u
    h_ref[...] = h


def last_kernel(
    scale0, scale1, scale2, scale3, x_ref, dy_ref, g_ref, u_ref, h_ref, g12_ref, u12_ref, h12_ref, xp_ref, dyp_ref,
    got, swap, wg_ref, wu_ref, wd_ref, *refs,
):
    out_refs = refs[: 2 * NZ]
    xs, dys, x_part, dy_part, blocks = refs[2 * NZ :]
    tokens, width = x_ref.shape
    part = width // NY
    merge((got,), (swap,), xs, dys)
    take_part(x_ref, x_part, 0)
    take_part(dy_ref, dy_part, 0)
    take_part(xs, x_part, 3 * tokens)
    take_part(dys, dy_part, 3 * tokens)
    x_part[tokens : 3 * tokens, :] = xp_ref[...]
    dy_part[tokens : 3 * tokens, :] = dyp_ref[...]
    last = forward(xs[...], dys[...], wg_ref[...], wu_ref[...], wd_ref[...])
    rows = part // NZ
    half = blocks.shape[2]
    for m, (left, mine, pair, other) in enumerate(
        (
            (x_part, g_ref, g12_ref, last[0]),
            (x_part, u_ref, u12_ref, last[1]),
            (dy_part, h_ref, h12_ref, last[2]),
        )
    ):
        pieces = (mine[...], pair[:tokens], pair[tokens:], other)
        scaled = [
            (piece.astype(F32) * scale[0:1, 0:1]).astype(BF16)
            for piece, scale in zip(pieces, (scale0, scale1, scale2, scale3))
        ]
        grad = dot(left[...], jnp.concatenate(scaled, axis=0), ((0,), (0,)))
        lo, hi = m * rows, (m + 1) * rows
        for z in range(NZ):
            if lo < half:
                stop = min(hi, half)
                blocks[z, 0, lo:stop, :] = grad[z * rows : z * rows + stop - lo]
            if hi > half:
                start = max(lo, half)
                blocks[z, 1, start - half : hi - half, :] = grad[z * rows + start - lo : (z + 1) * rows]
    me = lax.axis_index("z")
    for z in range(NZ):
        owner = lax.rem(me + z, NZ)
        for i in range(2):
            out_refs[2 * z + i][...] = blocks[owner, i]


def add_kernel(a_ref, b_ref, out_ref):
    out_ref[...] = a_ref[...] + b_ref[...]


def finish_kernel(top0, top1, top2, low0, low1, low2, gate_ref, up_ref, down_ref):
    rows = gate_ref.shape[0]
    half = top0.shape[0]
    top = top0[...] + (top1[...] + top2[...])
    low = low0[...] + (low1[...] + low2[...])
    gate_ref[...] = top[:rows]
    up_ref[: half - rows, :] = top[rows:]
    up_ref[half - rows :, :] = low[: 2 * rows - half]
    down_ref[...] = low[2 * rows - half : 3 * rows - half]


def per_device(inputs, gate_weight, up_weight, down_weight, out_grad, later_norms):
    tokens, width = inputs.shape
    ff = gate_weight.shape[1]
    part = width // NY
    rows = part // NZ
    half_rows = -(-3 * rows // 16) * 8
    slice_rows = tokens // (NX * NC)
    weights = (gate_weight.T, up_weight.T, down_weight.T)

    def shape(*dims, dtype=F32):
        return jax.ShapeDtypeStruct(dims, dtype)

    def call(kernel, name, outs, scratch, macs, mib, *args, spaces=()):
        spaces = dict(spaces)
        vmem = pl.BlockSpec(memory_space=pltpu.VMEM)
        return pl.pallas_call(
            kernel,
            out_shape=outs,
            in_specs=[pl.BlockSpec(memory_space=spaces.get(i, pltpu.VMEM)) for i in range(len(args))],
            out_specs=jax.tree.map(lambda _: vmem, outs),
            scratch_shapes=scratch,
            compiler_params=pltpu.CompilerParams(vmem_limit_bytes=mib * 1024 * 1024),
            cost_estimate=pl.CostEstimate(
                flops=macs * 4 * tokens * width * ff,
                bytes_accessed=sum(a.size * a.dtype.itemsize for a in args) if macs else 0,
                transcendentals=0,
            ),
            name=name,
        )(*args)

    mine, token = call(
        prepare_kernel, "prepare", [shape(tokens, width), shape(8, 128)], [], 0, 4, inputs, out_grad
    )
    got = [shift(mine, "y", k) for k in (1, 3, 2)]

    hiddens = [shape(tokens, ff, dtype=BF16)] * 3
    group = shape(NX + 1, slice_rows, width)
    *own_back, keep, give, wg, wu, wd = call(
        own_kernel, "own_example", hiddens + [group] * 2 + [shape(ff, width, dtype=BF16)] * 3,
        [pltpu.VMEM((tokens, width), BF16)] * 2
        + [pltpu.VMEM((NX * NC, slice_rows, width), F32), pltpu.SemaphoreType.DMA((5,))],
        0, OWN_MIB, inputs, out_grad, *weights, shift(token, "core", 1),
        spaces=[(i, pl.ANY) for i in range(6)],
    )
    weights = (wg, wu, wd)
    one = shape(slice_rows + 8, width)
    first, *rest = call(
        spread_kernel, "input_spread", [one] * 4, [pltpu.VMEM(group.shape, F32)], 0, 4,
        keep, shift(give, "core", 1),
    )
    rest = [shift(a, "x", k) for a, k in zip(rest, (1, 3, 2))]
    input_grad, scale = call(
        functools.partial(gather_kernel, factor=math.sqrt(width * ff * NX * NC / (NY * NZ))),
        "input_sum", [shape(slice_rows, width, dtype=BF16), shape(8, 128)], [], 0, 2,
        first, *rest, later_norms,
        spaces=[(4, pltpu.SMEM)],
    )
    scales = [scale] + [shift(scale, "y", k) for k in (1, 3, 2)]

    got = [after(a, t) for a, t in zip(got, (rest[2], rest[2], scale))]
    swapped = [shift(a, "core", 1) for a in got]
    both = [shape(2 * tokens, ff, dtype=BF16)] * 3 + [shape(2 * tokens, part, dtype=BF16)] * 2
    pair_back = call(
        pair_kernel, "pair_examples", both, [pltpu.VMEM((2 * tokens, width), BF16)] * 2, 6, 16,
        *got[:2], *swapped[:2], *weights,
    )
    blocks = call(
        last_kernel, "group_gradients", [shape(half_rows, ff)] * (2 * NZ),
        [pltpu.VMEM((tokens, width), BF16)] * 2 + [pltpu.VMEM((NY * tokens, part), BF16)] * 2
        + [pltpu.VMEM((NZ, 2, half_rows, ff), F32)], 6, 20,
        *scales, inputs, out_grad, *own_back, *pair_back, got[2], swapped[2], *weights,
    )
    plan = ((0, 1, 4), (1, -1, 4), (1, 1, 3), (0, -1, 3))
    held = [blocks[2 * (d * n % NZ) + i] for i, d, n in plan]
    for step in range(4):
        for c, (i, d, n) in enumerate(plan):
            if step < n:
                held[c] = shift(held[c], "z", d)
                if step < n - 1:
                    held[c] = call(
                        add_kernel, "add_block", shape(half_rows, ff), [], 0, 4,
                        held[c], blocks[2 * (d * (n - 1 - step) % NZ) + i],
                    )
    grads = call(
        finish_kernel, "finish", [shape(rows, ff)] * 3, [], 0, 4,
        blocks[0], held[0], held[3], blocks[1], held[1], held[2],
    )
    return (input_grad, *grads)


def solution(mesh):
    fine = Mesh(mesh.devices.reshape(NY, NZ, NX, NC), ("y", "z", "x", "core"))
    dp, tensor = ("y", "z"), ("x", "core")
    in_specs = (
        P(dp, None),
        P(None, tensor),
        P(None, tensor),
        P(None, tensor),
        P(dp, None),
        P(dp),
    )
    out_specs = (P(dp + tensor, None), P(dp, tensor), P(dp, tensor), P(dp, tensor))
    return jax.shard_map(
        per_device, mesh=fine, in_specs=in_specs, out_specs=out_specs, check_vma=False
    )
```

```python
import functools
import math

import jax
import jax.numpy as jnp
from jax import lax
from jax.experimental import pallas as pl
from jax.experimental.pallas import tpu as pltpu
from jax.sharding import Mesh, PartitionSpec as P

CLIP_NORM = 1.8
GELU_C = 0.7978845608028654
NY, NZ, NX, NC = 4, 8, 4, 2
OWN_MIB = 48
PREP_MIB = 56
F32 = jnp.float32
BF16 = jnp.bfloat16


def gelu_parts(pre):
    tangent = jnp.tanh(GELU_C * (pre + 0.044715 * pre * pre * pre))
    activated = 0.5 * pre * (1.0 + tangent)
    gelu_slope = 0.5 * (1.0 + tangent) + 0.5 * pre * (1.0 - tangent * tangent) * GELU_C * (
        1.0 + 3.0 * 0.044715 * pre * pre
    )
    return (activated, gelu_slope)


def shift(array, axis, step):
    size = lax.axis_size(axis)
    return lax.ppermute(array, axis, [(i, (i + step) % size) for i in range(size)])


def dot(left, right, dims):
    return lax.dot_general(left, right, (dims, ((), ())), preferred_element_type=F32)


def forward(x, dy, gate_weight, up_weight, down_weight):
    gate_pre = dot(x, gate_weight, ((1,), (1,)))
    up_pre = dot(x, up_weight, ((1,), (1,)))
    activated, gelu_slope = gelu_parts(gate_pre)
    hidden = (activated * up_pre).astype(BF16)
    hidden_grad = dot(dy, down_weight, ((1,), (1,)))
    gate_back = (hidden_grad * up_pre * gelu_slope).astype(BF16)
    up_back = (hidden_grad * activated).astype(BF16)
    return gate_back, up_back, hidden


def gram(matrix):
    return dot(matrix, matrix, ((1,), (1,)))


def prepare_kernel(x_ref, dy_ref, mine_ref, x_out, dy_out):
    x_out[...] = x_ref[...]
    dy_out[...] = dy_ref[...]
    first = lax.axis_index("core") == 0

    @pl.when(first)
    def _():
        mine_ref[...] = x_ref[...].astype(F32)

    @pl.when(jnp.logical_not(first))
    def _():
        mine_ref[...] = dy_ref[...].astype(F32)


def own_kernel(
    x_ref, dy_ref, wg_hbm, wu_hbm, wd_hbm, g_ref, u_ref, h_ref, keep_ref, give_ref, wg, wu, wd, rows_ref, sems
):
    pairs = ((wg_hbm, wg), (wu_hbm, wu), (wd_hbm, wd))
    copies = [pltpu.make_async_copy(a, b, sems.at[i]) for i, (a, b) in enumerate(pairs)]
    for copy in copies:
        copy.start()
    x = x_ref[...]
    dy = dy_ref[...]
    gram_x = gram(x)
    gram_dy = gram(dy)
    copies[0].wait()
    gate_pre = dot(x, wg[...], ((1,), (1,)))
    activated, gelu_slope = gelu_parts(gate_pre)
    copies[1].wait()
    up_pre = dot(x, wu[...], ((1,), (1,)))
    h = (activated * up_pre).astype(BF16)
    copies[2].wait()
    hidden_grad = dot(dy, wd[...], ((1,), (1,)))
    g = (hidden_grad * up_pre * gelu_slope).astype(BF16)
    u = (hidden_grad * activated).astype(BF16)
    g_ref[...] = g
    u_ref[...] = u
    h_ref[...] = h
    own = jnp.sum(gram_x * (gram(g) + gram(u)) + gram_dy * gram(h))
    total = dot(g, wg[...], ((1,), (0,))) + dot(u, wu[...], ((1,), (0,)))
    rows_ref[...] = total.reshape(rows_ref.shape)
    core = lax.axis_index("core")
    for i in range(NX):
        keep_ref[i] = rows_ref[NC * i + core]
        give_ref[i] = rows_ref[NC * i + 1 - core]
    for ref in (keep_ref, give_ref):
        ref[NX] = jnp.full(ref.shape[1:], own, F32)


def spread_kernel(keep_ref, got_ref, mine_ref, out1, out3, out2, rows_ref):
    rows_ref[...] = keep_ref[...] + got_ref[...]
    x = lax.axis_index("x")
    size = rows_ref.shape[1]
    for step, out_ref in ((0, mine_ref), (1, out1), (3, out3), (2, out2)):
        out_ref[:size, :] = rows_ref[lax.rem(x + step, NX)]
        out_ref[size:, :] = rows_ref[NX, :8, :]


def gather_kernel(mine_ref, got1, got3, got2, later_ref, input_ref, scale_ref, *, factor):
    total = mine_ref[...] + (got1[...] + got3[...]) + got2[...]
    size = input_ref.shape[0]
    input_ref[...] = total[:size].astype(BF16)
    own = total[size:, :128]
    scale_ref[...] = jnp.minimum(1.0, CLIP_NORM / jnp.sqrt(later_ref[0] + own)) * factor


def forward_kernel(up_ref, down_ref, token_ref, up_out, down_out, low_ref, high_ref):
    half = low_ref.shape[0]
    low_ref[...] = up_ref[:half]
    high_ref[...] = down_ref[half:]


def order_kernel(*refs):
    pass


def after(token, *arrays):
    hbm = pl.BlockSpec(memory_space=pl.ANY)
    return pl.pallas_call(
        order_kernel,
        out_shape=[jax.ShapeDtypeStruct(a.shape, a.dtype) for a in arrays],
        in_specs=[hbm] * (len(arrays) + 1),
        out_specs=[hbm] * len(arrays),
        input_output_aliases={i: i for i in range(len(arrays))},
        compiler_params=pltpu.CompilerParams(vmem_limit_bytes=1024 * 1024),
        name="order",
    )(*arrays, token)


def merge(got_refs, swap_refs, xs, dys):
    first = lax.axis_index("core") == 0
    row = 0
    for got_ref, swap_ref in zip(got_refs, swap_refs):
        rows = slice(row, row + got_ref.shape[0])
        row += got_ref.shape[0]

        @pl.when(first)
        def _():
            xs[rows, :] = got_ref[...].astype(BF16)
            dys[rows, :] = swap_ref[...].astype(BF16)

        @pl.when(jnp.logical_not(first))
        def _():
            xs[rows, :] = swap_ref[...].astype(BF16)
            dys[rows, :] = got_ref[...].astype(BF16)


def take_part(source_ref, target_ref, offset):
    tokens, width = source_ref.shape
    part = width // NY
    y = lax.axis_index("y")
    for k in range(NY):

        @pl.when(y == k)
        def _():
            target_ref[offset : offset + tokens, :] = source_ref[:, k * part : (k + 1) * part]


def pair_kernel(*refs):
    got, swap = refs[:2], refs[2:4]
    wg_ref, wu_ref, wd_ref, g_ref, u_ref, h_ref, xp_ref, dyp_ref, xs, dys = refs[4:]
    merge(got, swap, xs, dys)
    take_part(xs, xp_ref, 0)
    take_part(dys, dyp_ref, 0)
    g, u, h = forward(xs[...], dys[...], wg_ref[...], wu_ref[...], wd_ref[...])
    g_ref[...] = g
    u_ref[...] = u
    h_ref[...] = h


def last_kernel(
    scale0, scale1, scale2, scale3, x_ref, dy_ref, g_ref, u_ref, h_ref, g12_ref, u12_ref, h12_ref, xp_ref, dyp_ref,
    got0, got1, swap0, swap1, wg_ref, wu_ref, wd_ref, *refs,
):
    out_refs = refs[: 2 * NZ]
    xs, dys, x_part, dy_part, blocks = refs[2 * NZ :]
    tokens, width = x_ref.shape
    part = width // NY
    merge((got0, got1), (swap0, swap1), xs, dys)
    take_part(x_ref, x_part, 0)
    take_part(dy_ref, dy_part, 0)
    take_part(xs, x_part, 3 * tokens)
    take_part(dys, dy_part, 3 * tokens)
    x_part[tokens : 3 * tokens, :] = xp_ref[...]
    dy_part[tokens : 3 * tokens, :] = dyp_ref[...]
    last = forward(xs[...], dys[...], wg_ref[...], wu_ref[...], wd_ref[...])
    rows = part // NZ
    half = blocks.shape[2]
    for m, (left, mine, pair, other) in enumerate(
        (
            (x_part, g_ref, g12_ref, last[0]),
            (x_part, u_ref, u12_ref, last[1]),
            (dy_part, h_ref, h12_ref, last[2]),
        )
    ):
        pieces = (mine[...], pair[:tokens], pair[tokens:], other)
        scaled = [
            (piece.astype(F32) * scale[0:1, 0:1]).astype(BF16)
            for piece, scale in zip(pieces, (scale0, scale1, scale2, scale3))
        ]
        grad = dot(left[...], jnp.concatenate(scaled, axis=0), ((0,), (0,)))
        lo, hi = m * rows, (m + 1) * rows
        for z in range(NZ):
            if lo < half:
                stop = min(hi, half)
                blocks[z, 0, lo:stop, :] = grad[z * rows : z * rows + stop - lo]
            if hi > half:
                start = max(lo, half)
                blocks[z, 1, start - half : hi - half, :] = grad[z * rows + start - lo : (z + 1) * rows]
    me = lax.axis_index("z")
    for z in range(NZ):
        owner = lax.rem(me + z, NZ)
        for i in range(2):
            out_refs[2 * z + i][...] = blocks[owner, i]


def add_kernel(a_ref, b_ref, out_ref):
    out_ref[...] = a_ref[...] + b_ref[...]


def finish_kernel(top0, top1, top2, low0, low1, low2, gate_ref, up_ref, down_ref):
    rows = gate_ref.shape[0]
    half = top0.shape[0]
    top = top0[...] + (top1[...] + top2[...])
    low = low0[...] + (low1[...] + low2[...])
    gate_ref[...] = top[:rows]
    up_ref[: half - rows, :] = top[rows:]
    up_ref[half - rows :, :] = low[: 2 * rows - half]
    down_ref[...] = low[2 * rows - half : 3 * rows - half]


def per_device(inputs, gate_weight, up_weight, down_weight, out_grad, later_norms):
    tokens, width = inputs.shape
    ff = gate_weight.shape[1]
    part = width // NY
    rows = part // NZ
    half_rows = -(-3 * rows // 16) * 8
    slice_rows = tokens // (NX * NC)
    weights = (gate_weight.T, up_weight.T, down_weight.T)

    def shape(*dims, dtype=F32):
        return jax.ShapeDtypeStruct(dims, dtype)

    def call(kernel, name, outs, scratch, macs, mib, *args, spaces=()):
        spaces = dict(spaces)
        vmem = pl.BlockSpec(memory_space=pltpu.VMEM)
        return pl.pallas_call(
            kernel,
            out_shape=outs,
            in_specs=[pl.BlockSpec(memory_space=spaces.get(i, pltpu.VMEM)) for i in range(len(args))],
            out_specs=jax.tree.map(lambda _: vmem, outs),
            scratch_shapes=scratch,
            compiler_params=pltpu.CompilerParams(vmem_limit_bytes=mib * 1024 * 1024),
            cost_estimate=pl.CostEstimate(
                flops=macs * 4 * tokens * width * ff,
                bytes_accessed=sum(a.size * a.dtype.itemsize for a in args) if macs else 0,
                transcendentals=0,
            ),
            name=name,
        )(*args)

    inside = shape(tokens, width, dtype=BF16)
    mine, inputs, out_grad = call(
        prepare_kernel, "prepare", [shape(tokens, width), inside, inside], [], 0, PREP_MIB, inputs, out_grad
    )
    up, down = shift(mine, "y", 1), shift(mine, "y", -1)

    hiddens = [shape(tokens, ff, dtype=BF16)] * 3
    group = shape(NX + 1, slice_rows, width)
    *own_back, keep, give, wg, wu, wd = call(
        own_kernel, "own_example", hiddens + [group] * 2 + [shape(ff, width, dtype=BF16)] * 3,
        [pltpu.VMEM((NX * NC, slice_rows, width), F32), pltpu.SemaphoreType.DMA((3,))],
        0, OWN_MIB, inputs, out_grad, *weights, spaces=[(i, pl.ANY) for i in (2, 3, 4)],
    )
    weights = (wg, wu, wd)
    one = shape(slice_rows + 8, width)
    first, *rest = call(
        spread_kernel, "input_spread", [one] * 4, [pltpu.VMEM(group.shape, F32)], 0, 4,
        keep, shift(give, "core", 1),
    )
    rest = [shift(a, "x", k) for a, k in zip(rest, (1, 3, 2))]
    input_grad, scale = call(
        functools.partial(gather_kernel, factor=math.sqrt(width * ff * NX * NC / (NY * NZ))),
        "input_sum", [shape(slice_rows, width, dtype=BF16), shape(8, 128)], [], 0, 2,
        first, *rest, later_norms,
        spaces=[(4, pltpu.SMEM)],
    )
    scales = [scale] + [shift(scale, "y", k) for k in (1, 3, 2)]

    half = shape(tokens // 2, width)
    any_space = pl.BlockSpec(memory_space=pl.ANY)
    vmem_space = pl.BlockSpec(memory_space=pltpu.VMEM)
    up, down, low, high = pl.pallas_call(
        forward_kernel,
        out_shape=[shape(tokens, width), shape(tokens, width), half, half],
        in_specs=[vmem_space, vmem_space, any_space],
        out_specs=[vmem_space, vmem_space, vmem_space, vmem_space],
        input_output_aliases={0: 0, 1: 1},
        compiler_params=pltpu.CompilerParams(vmem_limit_bytes=8 * 1024 * 1024),
        name="forward",
    )(up, down, give)
    far = [shift(low, "y", 1), shift(high, "y", -1)]
    near = after(rest[2], up, down)
    near_swap = [shift(a, "core", 1) for a in near]
    far_swap = [shift(a, "core", 1) for a in far]
    both = [shape(2 * tokens, ff, dtype=BF16)] * 3 + [shape(2 * tokens, part, dtype=BF16)] * 2
    pair_back = call(
        pair_kernel, "pair_examples", both, [pltpu.VMEM((2 * tokens, width), BF16)] * 2, 6, 16,
        *near, *near_swap, *weights,
    )
    blocks = call(
        last_kernel, "group_gradients", [shape(half_rows, ff)] * (2 * NZ),
        [pltpu.VMEM((tokens, width), BF16)] * 2 + [pltpu.VMEM((NY * tokens, part), BF16)] * 2
        + [pltpu.VMEM((NZ, 2, half_rows, ff), F32)], 6, 20,
        *scales, inputs, out_grad, *own_back, *pair_back, *far, *far_swap, *weights,
    )
    plan = ((0, 1, 4), (1, -1, 4), (1, 1, 3), (0, -1, 3))
    held = [blocks[2 * (d * n % NZ) + i] for i, d, n in plan]
    for step in range(4):
        for c, (i, d, n) in enumerate(plan):
            if step < n:
                held[c] = shift(held[c], "z", d)
                if step < n - 1:
                    held[c] = call(
                        add_kernel, "add_block", shape(half_rows, ff), [], 0, 4,
                        held[c], blocks[2 * (d * (n - 1 - step) % NZ) + i],
                    )
    grads = call(
        finish_kernel, "finish", [shape(rows, ff)] * 3, [], 0, 4,
        blocks[0], held[0], held[3], blocks[1], held[1], held[2],
    )
    return (input_grad, *grads)


def solution(mesh):
    fine = Mesh(mesh.devices.reshape(NY, NZ, NX, NC), ("y", "z", "x", "core"))
    dp, tensor = ("y", "z"), ("x", "core")
    in_specs = (
        P(dp, None),
        P(None, tensor),
        P(None, tensor),
        P(None, tensor),
        P(dp, None),
        P(dp),
    )
    out_specs = (P(dp + tensor, None), P(dp, tensor), P(dp, tensor), P(dp, tensor))
    return jax.shard_map(
        per_device, mesh=fine, in_specs=in_specs, out_specs=out_specs, check_vma=False
    )
```

```python
import functools
import math

import jax
import jax.numpy as jnp
from jax import lax
from jax.experimental import pallas as pl
from jax.experimental.pallas import tpu as pltpu
from jax.sharding import Mesh, PartitionSpec as P

CLIP_NORM = 1.8
GELU_C = 0.7978845608028654
NY, NZ, NX, NC = 4, 8, 4, 2
OWN_MIB = 48
PREP_MIB = 8
F32 = jnp.float32
BF16 = jnp.bfloat16


def gelu_parts(pre):
    tangent = jnp.tanh(GELU_C * (pre + 0.044715 * pre * pre * pre))
    activated = 0.5 * pre * (1.0 + tangent)
    gelu_slope = 0.5 * (1.0 + tangent) + 0.5 * pre * (1.0 - tangent * tangent) * GELU_C * (
        1.0 + 3.0 * 0.044715 * pre * pre
    )
    return (activated, gelu_slope)


def shift(array, axis, step):
    size = lax.axis_size(axis)
    return lax.ppermute(array, axis, [(i, (i + step) % size) for i in range(size)])


def dot(left, right, dims):
    return lax.dot_general(left, right, (dims, ((), ())), preferred_element_type=F32)


def forward(x, dy, gate_weight, up_weight, down_weight):
    gate_pre = dot(x, gate_weight, ((1,), (1,)))
    up_pre = dot(x, up_weight, ((1,), (1,)))
    activated, gelu_slope = gelu_parts(gate_pre)
    hidden = (activated * up_pre).astype(BF16)
    hidden_grad = dot(dy, down_weight, ((1,), (1,)))
    gate_back = (hidden_grad * up_pre * gelu_slope).astype(BF16)
    up_back = (hidden_grad * activated).astype(BF16)
    return gate_back, up_back, hidden


def gram(matrix):
    return dot(matrix, matrix, ((1,), (1,)))


def prepare_kernel(x_ref, dy_ref, mine_ref, x_out, dy_out):
    x_out[...] = x_ref[...]
    dy_out[...] = dy_ref[...]
    first = lax.axis_index("core") == 0

    @pl.when(first)
    def _():
        mine_ref[...] = x_ref[...].astype(F32)

    @pl.when(jnp.logical_not(first))
    def _():
        mine_ref[...] = dy_ref[...].astype(F32)


def own_kernel(
    x_ref, dy_ref, wg_hbm, wu_hbm, wd_hbm, g_ref, u_ref, h_ref, keep_ref, give_ref, wg, wu, wd, rows_ref, sems
):
    pairs = ((wg_hbm, wg), (wu_hbm, wu), (wd_hbm, wd))
    copies = [pltpu.make_async_copy(a, b, sems.at[i]) for i, (a, b) in enumerate(pairs)]
    for copy in copies:
        copy.start()
    x = x_ref[...]
    dy = dy_ref[...]
    gram_x = gram(x)
    gram_dy = gram(dy)
    copies[0].wait()
    gate_pre = dot(x, wg[...], ((1,), (1,)))
    activated, gelu_slope = gelu_parts(gate_pre)
    copies[1].wait()
    up_pre = dot(x, wu[...], ((1,), (1,)))
    h = (activated * up_pre).astype(BF16)
    copies[2].wait()
    hidden_grad = dot(dy, wd[...], ((1,), (1,)))
    g = (hidden_grad * up_pre * gelu_slope).astype(BF16)
    u = (hidden_grad * activated).astype(BF16)
    g_ref[...] = g
    u_ref[...] = u
    h_ref[...] = h
    own = jnp.sum(gram_x * (gram(g) + gram(u)) + gram_dy * gram(h))
    total = dot(g, wg[...], ((1,), (0,))) + dot(u, wu[...], ((1,), (0,)))
    rows_ref[...] = total.reshape(rows_ref.shape)
    core = lax.axis_index("core")
    for i in range(NX):
        keep_ref[i] = rows_ref[NC * i + core]
        give_ref[i] = rows_ref[NC * i + 1 - core]
    for ref in (keep_ref, give_ref):
        ref[NX] = jnp.full(ref.shape[1:], own, F32)


def spread_kernel(keep_ref, got_ref, mine_ref, out1, out3, out2, rows_ref):
    rows_ref[...] = keep_ref[...] + got_ref[...]
    x = lax.axis_index("x")
    size = rows_ref.shape[1]
    for step, out_ref in ((0, mine_ref), (1, out1), (3, out3), (2, out2)):
        out_ref[:size, :] = rows_ref[lax.rem(x + step, NX)]
        out_ref[size:, :] = rows_ref[NX, :8, :]


def gather_kernel(mine_ref, got1, got3, got2, later_ref, token_ref, input_ref, scale_ref, *, factor):
    total = mine_ref[...] + (got1[...] + got3[...]) + got2[...]
    size = input_ref.shape[0]
    input_ref[...] = total[:size].astype(BF16)
    own = total[size:, :128]
    scale_ref[...] = jnp.minimum(1.0, CLIP_NORM / jnp.sqrt(later_ref[0] + own)) * factor


def forward_kernel(up_ref, down_ref, token_ref, up_out, down_out, low_ref, high_ref):
    half = low_ref.shape[0]
    low_ref[...] = up_ref[:half]
    high_ref[...] = down_ref[half:]


def order_kernel(*refs):
    pass


def after(token, *arrays):
    hbm = pl.BlockSpec(memory_space=pl.ANY)
    return pl.pallas_call(
        order_kernel,
        out_shape=[jax.ShapeDtypeStruct(a.shape, a.dtype) for a in arrays],
        in_specs=[hbm] * (len(arrays) + 1),
        out_specs=[hbm] * len(arrays),
        input_output_aliases={i: i for i in range(len(arrays))},
        compiler_params=pltpu.CompilerParams(vmem_limit_bytes=1024 * 1024),
        name="order",
    )(*arrays, token)


def merge(got_refs, swap_refs, xs, dys):
    first = lax.axis_index("core") == 0
    row = 0
    for got_ref, swap_ref in zip(got_refs, swap_refs):
        rows = slice(row, row + got_ref.shape[0])
        row += got_ref.shape[0]

        @pl.when(first)
        def _():
            xs[rows, :] = got_ref[...].astype(BF16)
            dys[rows, :] = swap_ref[...].astype(BF16)

        @pl.when(jnp.logical_not(first))
        def _():
            xs[rows, :] = swap_ref[...].astype(BF16)
            dys[rows, :] = got_ref[...].astype(BF16)


def take_part(source_ref, target_ref, offset):
    tokens, width = source_ref.shape
    part = width // NY
    y = lax.axis_index("y")
    for k in range(NY):

        @pl.when(y == k)
        def _():
            target_ref[offset : offset + tokens, :] = source_ref[:, k * part : (k + 1) * part]


def group_kernel(
    scale0, scale1, scale2, scale3, x_ref, dy_ref, g_ref, u_ref, h_ref, got0, got1, got2, got3,
    swap0, swap1, swap2, swap3, wg_ref, wu_ref, wd_ref, *refs,
):
    out_refs = refs[: 2 * NZ]
    xs, dys, x_part, dy_part, blocks = refs[2 * NZ :]
    tokens, width = x_ref.shape
    part = width // NY
    merge((got0, got1, got2, got3), (swap0, swap1, swap2, swap3), xs, dys)
    take_part(x_ref, x_part, 0)
    take_part(dy_ref, dy_part, 0)
    take_part(xs, x_part, tokens)
    take_part(dys, dy_part, tokens)
    others = forward(xs[...], dys[...], wg_ref[...], wu_ref[...], wd_ref[...])
    rows = part // NZ
    half = blocks.shape[2]
    for m, (left, mine, other) in enumerate(
        ((x_part, g_ref, others[0]), (x_part, u_ref, others[1]), (dy_part, h_ref, others[2]))
    ):
        pieces = [mine[...]] + [other[e * tokens : (e + 1) * tokens] for e in range(NY - 1)]
        scaled = [
            (piece.astype(F32) * scale[0:1, 0:1]).astype(BF16)
            for piece, scale in zip(pieces, (scale0, scale1, scale2, scale3))
        ]
        grad = dot(left[...], jnp.concatenate(scaled, axis=0), ((0,), (0,)))
        lo, hi = m * rows, (m + 1) * rows
        for z in range(NZ):
            if lo < half:
                stop = min(hi, half)
                blocks[z, 0, lo:stop, :] = grad[z * rows : z * rows + stop - lo]
            if hi > half:
                start = max(lo, half)
                blocks[z, 1, start - half : hi - half, :] = grad[z * rows + start - lo : (z + 1) * rows]
    me = lax.axis_index("z")
    for z in range(NZ):
        owner = lax.rem(me + z, NZ)
        for i in range(2):
            out_refs[2 * z + i][...] = blocks[owner, i]


def add_kernel(a_ref, b_ref, out_ref):
    out_ref[...] = a_ref[...] + b_ref[...]


def finish_kernel(top0, top1, top2, low0, low1, low2, gate_ref, up_ref, down_ref):
    rows = gate_ref.shape[0]
    half = top0.shape[0]
    top = top0[...] + (top1[...] + top2[...])
    low = low0[...] + (low1[...] + low2[...])
    gate_ref[...] = top[:rows]
    up_ref[: half - rows, :] = top[rows:]
    up_ref[half - rows :, :] = low[: 2 * rows - half]
    down_ref[...] = low[2 * rows - half : 3 * rows - half]


def per_device(inputs, gate_weight, up_weight, down_weight, out_grad, later_norms):
    tokens, width = inputs.shape
    ff = gate_weight.shape[1]
    part = width // NY
    rows = part // NZ
    half_rows = -(-3 * rows // 16) * 8
    slice_rows = tokens // (NX * NC)
    weights = (gate_weight.T, up_weight.T, down_weight.T)

    def shape(*dims, dtype=F32):
        return jax.ShapeDtypeStruct(dims, dtype)

    def call(kernel, name, outs, scratch, macs, mib, *args, spaces=()):
        spaces = dict(spaces)
        vmem = pl.BlockSpec(memory_space=pltpu.VMEM)
        return pl.pallas_call(
            kernel,
            out_shape=outs,
            in_specs=[pl.BlockSpec(memory_space=spaces.get(i, pltpu.VMEM)) for i in range(len(args))],
            out_specs=jax.tree.map(lambda _: vmem, outs),
            scratch_shapes=scratch,
            compiler_params=pltpu.CompilerParams(vmem_limit_bytes=mib * 1024 * 1024),
            cost_estimate=pl.CostEstimate(
                flops=macs * 4 * tokens * width * ff,
                bytes_accessed=sum(a.size * a.dtype.itemsize for a in args) if macs else 0,
                transcendentals=0,
            ),
            name=name,
        )(*args)

    inside = shape(tokens, width, dtype=BF16)
    mine, inputs, out_grad = call(
        prepare_kernel, "prepare", [shape(tokens, width), inside, inside], [], 0, PREP_MIB, inputs, out_grad
    )
    up, down = shift(mine, "y", 1), shift(mine, "y", -1)

    hiddens = [shape(tokens, ff, dtype=BF16)] * 3
    group = shape(NX + 1, slice_rows, width)
    *own_back, keep, give, wg, wu, wd = call(
        own_kernel, "own_example", hiddens + [group] * 2 + [shape(ff, width, dtype=BF16)] * 3,
        [pltpu.VMEM((NX * NC, slice_rows, width), F32), pltpu.SemaphoreType.DMA((3,))],
        0, OWN_MIB, inputs, out_grad, *weights, spaces=[(i, pl.ANY) for i in (2, 3, 4)],
    )
    weights = (wg, wu, wd)
    one = shape(slice_rows + 8, width)
    first, *rest = call(
        spread_kernel, "input_spread", [one] * 4, [pltpu.VMEM(group.shape, F32)], 0, 4,
        keep, shift(give, "core", 1),
    )
    half = shape(tokens // 2, width)
    any_space = pl.BlockSpec(memory_space=pl.ANY)
    vmem_space = pl.BlockSpec(memory_space=pltpu.VMEM)
    up, down, low, high = pl.pallas_call(
        forward_kernel,
        out_shape=[shape(tokens, width), shape(tokens, width), half, half],
        in_specs=[vmem_space, vmem_space, any_space],
        out_specs=[vmem_space, vmem_space, vmem_space, vmem_space],
        input_output_aliases={0: 0, 1: 1},
        compiler_params=pltpu.CompilerParams(vmem_limit_bytes=8 * 1024 * 1024),
        name="forward",
    )(up, down, give)
    far = [shift(low, "y", 1), shift(high, "y", -1)]
    rest = [shift(a, "x", k) for a, k in zip(rest, (1, 3, 2))]
    input_grad, scale = call(
        functools.partial(gather_kernel, factor=math.sqrt(width * ff * NX * NC / (NY * NZ))),
        "input_sum", [shape(slice_rows, width, dtype=BF16), shape(8, 128)], [], 0, 2,
        first, *rest, later_norms, low,
        spaces=[(4, pltpu.SMEM), (5, pl.ANY)],
    )
    scales = [scale] + [shift(scale, "y", k) for k in (1, 3, 2)]

    near = after(scales[1], up, down)
    near_swap = [shift(a, "core", 1) for a in near]
    far = after(scales[3], *far)
    far_swap = [shift(a, "core", 1) for a in far]
    blocks = call(
        group_kernel, "group_gradients", [shape(half_rows, ff)] * (2 * NZ),
        [pltpu.VMEM(((NY - 1) * tokens, width), BF16)] * 2 + [pltpu.VMEM((NY * tokens, part), BF16)] * 2
        + [pltpu.VMEM((NZ, 2, half_rows, ff), F32)], 12, 24,
        *scales, inputs, out_grad, *own_back, *near, *far, *near_swap, *far_swap, *weights,
    )
    plan = ((0, 1, 4), (1, -1, 4), (1, 1, 3), (0, -1, 3))
    held = [blocks[2 * (d * n % NZ) + i] for i, d, n in plan]
    for step in range(4):
        for c, (i, d, n) in enumerate(plan):
            if step < n:
                held[c] = shift(held[c], "z", d)
                if step < n - 1:
                    held[c] = call(
                        add_kernel, "add_block", shape(half_rows, ff), [], 0, 4,
                        held[c], blocks[2 * (d * (n - 1 - step) % NZ) + i],
                    )
    grads = call(
        finish_kernel, "finish", [shape(rows, ff)] * 3, [], 0, 4,
        blocks[0], held[0], held[3], blocks[1], held[1], held[2],
    )
    return (input_grad, *grads)


def solution(mesh):
    fine = Mesh(mesh.devices.reshape(NY, NZ, NX, NC), ("y", "z", "x", "core"))
    dp, tensor = ("y", "z"), ("x", "core")
    in_specs = (
        P(dp, None),
        P(None, tensor),
        P(None, tensor),
        P(None, tensor),
        P(dp, None),
        P(dp),
    )
    out_specs = (P(dp + tensor, None), P(dp, tensor), P(dp, tensor), P(dp, tensor))
    return jax.shard_map(
        per_device, mesh=fine, in_specs=in_specs, out_specs=out_specs, check_vma=False
    )
```
